32 devices in a mesh: lat: 4 (over x, core), lon: 8 (over z, y).
Axes of the slice: x: 2, y: 2, z: 4, core: 2. Of those that a mesh axis runs over, the one named last changes fastest.
Arguments:
- field: bfloat16 [1440, 720, 256], P('lon', 'lat'), may hold values from -6 to 6
- cotangent: bfloat16 [1440, 720, 256], P('lon', 'lat'), may hold values from -6 to 6
- spectral_filter: bfloat16 [2, 720, 256], P(None, None, 'lon'), may hold values from -4 to 4
Outputs:
- output: bfloat16 [1440, 720, 256], P('lon', 'lat')
- grad_field: bfloat16 [1440, 720, 256], P('lon', 'lat')
- grad_filter: float32 [2, 720, 256], P(None, None, 'lon')
The draws below stay inside these ranges and needn't reach their ends.
All inputs are finite; a program needn't handle non-finite values.
Results may differ from the reference program's by a relative error of at most 0.024.
Values may be sent and summed in bfloat16 or wider, within the bound.
A program may use at most 192 MiB of HBM per device.

```python
import math
import jax
import jax.numpy as jnp
from jax import lax

C = 256
NLAT = 720
NLON = 1440
L = 720
M = 32


def shard_levels(key, shape, cuts, low, top_value):
    def one(position, parts):
        draws = jax.random.uniform(jax.random.fold_in(jax.random.fold_in(key, 6), position), (parts,), jnp.float32, low / len(cuts), top_value / len(cuts))
        return jnp.repeat(jnp.exp(draws), shape[position] // parts).reshape((-1,) + (1,) * (len(shape) - position - 1))

    factor_of = one(*cuts[0])
    for cut in cuts[1:]:
        factor_of = factor_of * one(*cut)
    return factor_of


def bell_draw(stream_key, dims, deviation, most, split=(), kind=jnp.bfloat16):
    drawn = deviation * jax.random.normal(stream_key, dims, jnp.float32)
    if split:
        drawn = drawn * shard_levels(stream_key, dims, split, -0.22, 0.18)
    return jnp.clip(drawn, -most, most).astype(kind)


def setup_inputs(seed: int = 0) -> dict:
    key_list = jax.random.split(jax.random.key(seed), 4)
    return {
        "field": bell_draw(key_list[0], (NLON, NLAT, C), 1.0, 6.0, ((0, 8), (1, 4))),
        "cotangent": bell_draw(key_list[1], (NLON, NLAT, C), 1.0, 6.0, ((0, 8), (1, 4))),
        "spectral_filter": bell_draw(key_list[2], (2, L, C), 0.7, 4.0, ((2, 8),)),
    }


def fourier_table(wave_count, points):
    wave_index = jnp.arange(wave_count, dtype=jnp.int32)
    point_index = jnp.arange(points, dtype=jnp.int32)
    phase_steps = wave_index[:, None] * point_index[None, :] % points
    angles = phase_steps.astype(jnp.float32) * (2.0 * math.pi / points)
    stacked = jnp.stack([jnp.cos(angles), -jnp.sin(angles)], axis=1)
    return stacked.reshape(2 * wave_count, points).astype(jnp.bfloat16)

def compose(earlier, latter):
    upper_left = latter[0] * earlier[0] + latter[1] * earlier[2]
    upper_right = latter[0] * earlier[1] + latter[1] * earlier[3]
    lower_left = latter[2] * earlier[0] + latter[3] * earlier[2]
    lower_right = latter[2] * earlier[1] + latter[3] * earlier[3]
    largest = jnp.maximum(jnp.maximum(jnp.abs(upper_left), jnp.abs(upper_right)), jnp.maximum(jnp.abs(lower_left), jnp.abs(lower_right)))
    return (upper_left / largest, upper_right / largest, lower_left / largest, lower_right / largest, earlier[4] + latter[4] + jnp.log(largest))

def legendre_pair(wave_order, lat_count, degree_count):
    order_value = wave_order.astype(jnp.float32)
    degrees = jnp.arange(degree_count, dtype=jnp.float32)
    beyond = degrees > order_value
    numerator = jnp.where(beyond, 4.0 * degrees * degrees - 1.0, 1.0)
    denominator = jnp.where(beyond, degrees * degrees - order_value * order_value, 1.0)
    factor = jnp.sqrt(numerator / denominator)
    earlier_factor = jnp.concatenate([jnp.ones((1,), jnp.float32), factor[:-1]])
    subdiagonal = jnp.where(degrees > order_value + 1.0, -factor / earlier_factor, 0.0)
    start_log = 0.5 * (lax.lgamma(order_value + 1.5) - lax.lgamma(jnp.float32(1.5)) - lax.lgamma(order_value + 1.0)) - 0.5 * math.log(4.0 * math.pi)
    colatitude = (jnp.arange(lat_count, dtype=jnp.float32) + 0.5) * (math.pi / lat_count)
    cosine = jnp.cos(colatitude)[None, :]
    sines = jnp.sin(colatitude)
    block_len = 16
    block_count = degree_count // block_len
    grid_shape = (block_count, lat_count)

    def picked(values, step):
        return values.reshape(block_count, block_len)[:, step][:, None]

    def element(step):
        inside = picked(beyond, step)
        return (jnp.where(inside, 0.0, 1.0).astype(jnp.float32), jnp.where(inside, 1.0, 0.0).astype(jnp.float32), picked(subdiagonal, step).astype(jnp.float32), jnp.where(inside, picked(factor, step) * cosine, 1.0).astype(jnp.float32), jnp.zeros((block_count, 1), jnp.float32))
    ones_grid = jnp.ones(grid_shape, jnp.float32)
    zeros_grid = jnp.zeros(grid_shape, jnp.float32)
    identity = (ones_grid, zeros_grid, zeros_grid, ones_grid, zeros_grid)
    totals = identity
    for step in range(block_len):
        totals = compose(totals, element(step))
    inclusive = lax.associative_scan(compose, totals, axis=0)
    carry = tuple((jnp.concatenate([first[:1], later[:-1]], axis=0) for first, later in zip(identity, inclusive)))
    lower_parts = []
    log_parts = []
    for step in range(block_len):
        carry = compose(carry, element(step))
        lower_parts.append(carry[3])
        log_parts.append(carry[4])
    lower_right = jnp.stack(lower_parts, axis=1).reshape(degree_count, lat_count)
    log_scale = jnp.stack(log_parts, axis=1).reshape(degree_count, lat_count)
    values = lower_right * jnp.exp(log_scale + start_log + order_value * jnp.log(sines)[None, :])
    functions = jnp.where((degrees >= order_value)[:, None], values, 0.0)
    weights = math.pi / lat_count * sines
    return (functions.astype(jnp.bfloat16), (functions * weights[None, :]).astype(jnp.bfloat16))

def spectral_products(weights, analysis, adjoint_synthesis):
    filter_real = weights[0]
    filter_imaginary = weights[1]
    real_part = filter_real * analysis[0] - filter_imaginary * analysis[1]
    imaginary_part = filter_real * analysis[1] + filter_imaginary * analysis[0]
    filtered = jnp.stack([real_part, imaginary_part]).astype(jnp.bfloat16)
    gradient_term = jnp.stack([analysis[0] * adjoint_synthesis[0] + analysis[1] * adjoint_synthesis[1], analysis[0] * adjoint_synthesis[1] - analysis[1] * adjoint_synthesis[0]])
    adjoint_filtered = jnp.stack([filter_real * adjoint_synthesis[0] + filter_imaginary * adjoint_synthesis[1], filter_real * adjoint_synthesis[1] - filter_imaginary * adjoint_synthesis[0]]).astype(jnp.bfloat16)
    return (filtered, gradient_term, adjoint_filtered)

def reference(field, cotangent, spectral_filter):
    highest = lax.Precision.HIGHEST
    fourier_rows = fourier_table(M, NLON).astype(jnp.float32)
    spacing = 2.0 * math.pi / NLON
    doubling = jnp.where(jnp.arange(2 * M) // 2 == 0, 1.0, 2.0).astype(jnp.float32)[:, None]
    weights = spectral_filter.astype(jnp.float32)

    def analyze(lat_row):
        return (jnp.dot(fourier_rows, lat_row.astype(jnp.float32), precision=highest) * spacing).astype(jnp.bfloat16)

    def adjoint_in(lat_row):
        return (jnp.dot(fourier_rows, lat_row.astype(jnp.float32), precision=highest) * doubling).astype(jnp.bfloat16)
    fourier = lax.map(analyze, jnp.transpose(field, (1, 0, 2)))
    adjoint_fourier = lax.map(adjoint_in, jnp.transpose(cotangent, (1, 0, 2)))
    fourier_modes = jnp.transpose(fourier.reshape(NLAT, M, 2, C), (1, 2, 0, 3))
    adjoint_modes = jnp.transpose(adjoint_fourier.reshape(NLAT, M, 2, C), (1, 2, 0, 3))

    def per_order(running, inputs):
        wave_order, fourier_spec, adjoint_spec = inputs
        legendre, weighted = legendre_pair(wave_order, NLAT, L)
        legendre = legendre.astype(jnp.float32)
        weighted = weighted.astype(jnp.float32)
        analysis = jnp.einsum('lj,rjc->rlc', weighted, fourier_spec.astype(jnp.float32), precision=highest)
        adjoint_synthesis = jnp.einsum('lj,rjc->rlc', legendre, adjoint_spec.astype(jnp.float32), precision=highest)
        filtered, gradient_term, adjoint_filtered = spectral_products(weights, analysis, adjoint_synthesis)
        synthesis = jnp.einsum('lj,rlc->rjc', legendre, filtered.astype(jnp.float32), precision=highest).astype(jnp.bfloat16)
        adjoint_analysis = jnp.einsum('lj,rlc->rjc', weighted, adjoint_filtered.astype(jnp.float32), precision=highest).astype(jnp.bfloat16)
        return (running + gradient_term, (synthesis, adjoint_analysis))
    grad_filter, (synthesis_modes, adjoint_modes_back) = lax.scan(per_order, jnp.zeros((2, L, C), jnp.float32), (jnp.arange(M, dtype=jnp.int32), fourier_modes, adjoint_modes))
    synthesis_rows = jnp.transpose(synthesis_modes, (2, 0, 1, 3)).reshape(NLAT, 2 * M, C)
    adjoint_rows = jnp.transpose(adjoint_modes_back, (2, 0, 1, 3)).reshape(NLAT, 2 * M, C)

    def synthesize(lat_row):
        return jnp.dot(fourier_rows.T, doubling * lat_row.astype(jnp.float32), precision=highest).astype(jnp.bfloat16)

    def adjoint_out(lat_row):
        return (jnp.dot(fourier_rows.T, lat_row.astype(jnp.float32), precision=highest) * spacing).astype(jnp.bfloat16)
    output = jnp.transpose(lax.map(synthesize, synthesis_rows), (1, 0, 2))
    grad_field = jnp.transpose(lax.map(adjoint_out, adjoint_rows), (1, 0, 2))
    return (output, grad_field, grad_filter)
```

```python
import math

import jax
import jax.numpy as jnp
from jax import lax
from jax.sharding import PartitionSpec as P


def fourier_table(wave_count, points):
    wave_index = jnp.arange(wave_count, dtype=jnp.int32)
    point_index = jnp.arange(points, dtype=jnp.int32)
    phase_steps = wave_index[:, None] * point_index[None, :] % points
    angles = phase_steps.astype(jnp.float32) * (2.0 * math.pi / points)
    stacked = jnp.stack([jnp.cos(angles), -jnp.sin(angles)], axis=1)
    return stacked.reshape(2 * wave_count, points).astype(jnp.bfloat16)


def compose(earlier, latter):
    upper_left = latter[0] * earlier[0] + latter[1] * earlier[2]
    upper_right = latter[0] * earlier[1] + latter[1] * earlier[3]
    lower_left = latter[2] * earlier[0] + latter[3] * earlier[2]
    lower_right = latter[2] * earlier[1] + latter[3] * earlier[3]
    largest = jnp.maximum(
        jnp.maximum(jnp.abs(upper_left), jnp.abs(upper_right)),
        jnp.maximum(jnp.abs(lower_left), jnp.abs(lower_right)),
    )
    return (
        upper_left / largest,
        upper_right / largest,
        lower_left / largest,
        lower_right / largest,
        earlier[4] + latter[4] + jnp.log(largest),
    )


def legendre_pair(wave_order, lat_count, degree_count):
    order_value = wave_order.astype(jnp.float32)
    degrees = jnp.arange(degree_count, dtype=jnp.float32)
    beyond = degrees > order_value
    numerator = jnp.where(beyond, 4.0 * degrees * degrees - 1.0, 1.0)
    denominator = jnp.where(beyond, degrees * degrees - order_value * order_value, 1.0)
    factor = jnp.sqrt(numerator / denominator)
    earlier_factor = jnp.concatenate([jnp.ones((1,), jnp.float32), factor[:-1]])
    subdiagonal = jnp.where(degrees > order_value + 1.0, -factor / earlier_factor, 0.0)
    start_log = 0.5 * (
        lax.lgamma(order_value + 1.5) - lax.lgamma(jnp.float32(1.5)) - lax.lgamma(order_value + 1.0)
    ) - 0.5 * math.log(4.0 * math.pi)
    colatitude = (jnp.arange(lat_count, dtype=jnp.float32) + 0.5) * (math.pi / lat_count)
    cosine = jnp.cos(colatitude)[None, :]
    sines = jnp.sin(colatitude)
    block_len = 16
    block_count = degree_count // block_len
    grid_shape = (block_count, lat_count)

    def picked(values, step):
        return values.reshape(block_count, block_len)[:, step][:, None]

    def element(step):
        inside = picked(beyond, step)
        return (
            jnp.where(inside, 0.0, 1.0).astype(jnp.float32),
            jnp.where(inside, 1.0, 0.0).astype(jnp.float32),
            picked(subdiagonal, step),
            jnp.where(inside, picked(factor, step) * cosine, 1.0),
            jnp.zeros((block_count, 1), jnp.float32),
        )

    ones_grid = jnp.ones(grid_shape, jnp.float32)
    zeros_grid = jnp.zeros(grid_shape, jnp.float32)
    identity = (ones_grid, zeros_grid, zeros_grid, ones_grid, zeros_grid)
    totals = identity
    for step in range(block_len):
        totals = compose(totals, element(step))
    inclusive = lax.associative_scan(compose, totals, axis=0)
    carry = tuple(
        (
            jnp.concatenate([first[:1], later[:-1]], axis=0)
            for first, later in zip(identity, inclusive)
        )
    )
    lower_parts = []
    log_parts = []
    for step in range(block_len):
        carry = compose(carry, element(step))
        lower_parts.append(carry[3])
        log_parts.append(carry[4])
    lower_right = jnp.stack(lower_parts, axis=1).reshape(degree_count, lat_count)
    log_scale = jnp.stack(log_parts, axis=1).reshape(degree_count, lat_count)
    values = lower_right * jnp.exp(log_scale + start_log + order_value * jnp.log(sines)[None, :])
    functions = jnp.where((degrees >= order_value)[:, None], values, 0.0)
    weights = math.pi / lat_count * sines
    return (functions.astype(jnp.bfloat16), (functions * weights[None, :]).astype(jnp.bfloat16))


def spectral_products(weights, analysis, adjoint_synthesis):
    filter_real = weights[0]
    filter_imaginary = weights[1]
    real_part = filter_real * analysis[0] - filter_imaginary * analysis[1]
    imaginary_part = filter_real * analysis[1] + filter_imaginary * analysis[0]
    filtered = jnp.stack([real_part, imaginary_part]).astype(jnp.bfloat16)
    gradient_term = jnp.stack(
        [
            analysis[0] * adjoint_synthesis[0] + analysis[1] * adjoint_synthesis[1],
            analysis[0] * adjoint_synthesis[1] - analysis[1] * adjoint_synthesis[0],
        ]
    )
    adjoint_filtered = jnp.stack(
        [
            filter_real * adjoint_synthesis[0] + filter_imaginary * adjoint_synthesis[1],
            filter_real * adjoint_synthesis[1] - filter_imaginary * adjoint_synthesis[0],
        ]
    ).astype(jnp.bfloat16)
    return (filtered, gradient_term, adjoint_filtered)


def spectral_work(legendre, weighted, weights, fourier_spec, adjoint_spec):
    analysis = jnp.einsum("lj,rjc->rlc", weighted, fourier_spec, preferred_element_type=jnp.float32)
    adjoint_synthesis = jnp.einsum(
        "lj,rjc->rlc", legendre, adjoint_spec, preferred_element_type=jnp.float32
    )
    filtered, gradient_term, adjoint_filtered = spectral_products(
        weights, analysis, adjoint_synthesis
    )
    synthesis = jnp.einsum(
        "lj,rlc->rjc", legendre, filtered, preferred_element_type=jnp.float32
    ).astype(jnp.bfloat16)
    adjoint_analysis = jnp.einsum(
        "lj,rlc->rjc", weighted, adjoint_filtered, preferred_element_type=jnp.float32
    ).astype(jnp.bfloat16)
    return (synthesis, adjoint_analysis, gradient_term)


def per_device(field, cotangent, spectral_filter):
    lat_count = lax.axis_size("lat")
    lon_count = lax.axis_size("lon")
    lon_local, lat_local, channels = field.shape
    points = lon_local * lon_count
    latitudes = lat_local * lat_count
    wave_count = lat_count * lon_count
    degree_count = spectral_filter.shape[1]
    channel_share = channels // lon_count
    own_lon = lax.axis_index("lon")
    spacing = 2.0 * math.pi / points
    local_rows = lax.dynamic_slice_in_dim(
        fourier_table(wave_count, points), own_lon * lon_local, lon_local, 1
    )
    doubling_rows = jnp.where(jnp.arange(2 * wave_count) // 2 == 0, 1.0, 2.0).astype(jnp.float32)[
        :, None, None
    ]
    wave_order = own_lon * lat_count + lax.axis_index("lat")
    legendre, weighted = legendre_pair(wave_order, latitudes, degree_count)
    weights = lax.all_gather(spectral_filter, "lon", axis=2, tiled=True).astype(jnp.float32)

    def to_spectral(grid, factor):
        partial = jnp.einsum("rn,njc->rjc", local_rows, grid, preferred_element_type=jnp.float32)
        partial = (partial * factor).astype(jnp.bfloat16)
        own = lax.psum_scatter(partial, "lon", scatter_dimension=0, tiled=True)
        own = own.reshape(lat_count, 2, lat_local, channels)
        moved = lax.all_to_all(own, "lat", split_axis=0, concat_axis=0, tiled=True)
        return jnp.transpose(moved, (1, 0, 2, 3)).reshape(2, latitudes, channels)

    def to_grid(spectra, factor):
        bands = jnp.transpose(spectra.reshape(2, lat_count, lat_local, channels), (1, 0, 2, 3))
        moved = lax.all_to_all(bands, "lat", split_axis=0, concat_axis=0, tiled=True)
        moved = moved.reshape(2 * lat_count, lat_local, channels)
        rows = lax.all_gather(moved, "lon", axis=0, tiled=True)
        grid = jnp.einsum("rn,rjc->njc", local_rows, rows, preferred_element_type=jnp.float32)
        return (grid * factor).astype(jnp.bfloat16)

    fourier_spec = to_spectral(field, spacing)
    adjoint_spec = to_spectral(cotangent, doubling_rows)
    synthesis, adjoint_analysis, gradient_term = spectral_work(
        legendre, weighted, weights, fourier_spec, adjoint_spec
    )
    doubled = jnp.where(wave_order == 0, 1.0, 2.0).astype(jnp.bfloat16)
    output = to_grid(synthesis * doubled, 1.0)
    grad_field = to_grid(adjoint_analysis, spacing)
    shares = jnp.transpose(
        gradient_term.reshape(2, degree_count, lon_count, channel_share), (2, 0, 1, 3)
    ).reshape(lon_count, -1)
    share = lax.psum(lax.psum_scatter(shares, "lon", scatter_dimension=0, tiled=True), "lat")
    grad_filter = share.reshape(2, degree_count, channel_share)
    return (output, grad_field, grad_filter)


def solution(mesh):
    in_specs = (P("lon", "lat", None), P("lon", "lat", None), P(None, None, "lon"))
    out_specs = (P("lon", "lat", None), P("lon", "lat", None), P(None, None, "lon"))
    return jax.shard_map(
        per_device, mesh=mesh, in_specs=in_specs, out_specs=out_specs, check_vma=False
    )
```

```python
import math

import jax
import jax.numpy as jnp
from jax import lax
from jax.experimental import pallas as pl
from jax.experimental.pallas import tpu as pltpu
from jax.sharding import PartitionSpec as P


def fourier_table(wave_count, points):
    wave_index = jnp.arange(wave_count, dtype=jnp.int32)
    point_index = jnp.arange(points, dtype=jnp.int32)
    phase_steps = wave_index[:, None] * point_index[None, :] % points
    angles = phase_steps.astype(jnp.float32) * (2.0 * math.pi / points)
    stacked = jnp.stack([jnp.cos(angles), -jnp.sin(angles)], axis=1)
    return stacked.reshape(2 * wave_count, points).astype(jnp.bfloat16)


def compose(earlier, latter):
    upper_left = latter[0] * earlier[0] + latter[1] * earlier[2]
    upper_right = latter[0] * earlier[1] + latter[1] * earlier[3]
    lower_left = latter[2] * earlier[0] + latter[3] * earlier[2]
    lower_right = latter[2] * earlier[1] + latter[3] * earlier[3]
    largest = jnp.maximum(
        jnp.maximum(jnp.abs(upper_left), jnp.abs(upper_right)),
        jnp.maximum(jnp.abs(lower_left), jnp.abs(lower_right)),
    )
    return (
        upper_left / largest,
        upper_right / largest,
        lower_left / largest,
        lower_right / largest,
        earlier[4] + latter[4] + jnp.log(largest),
    )


def legendre_pair(wave_order, lat_count, degree_count):
    order_value = wave_order.astype(jnp.float32)
    degrees = jnp.arange(degree_count, dtype=jnp.float32)
    beyond = degrees > order_value
    numerator = jnp.where(beyond, 4.0 * degrees * degrees - 1.0, 1.0)
    denominator = jnp.where(beyond, degrees * degrees - order_value * order_value, 1.0)
    factor = jnp.sqrt(numerator / denominator)
    earlier_factor = jnp.concatenate([jnp.ones((1,), jnp.float32), factor[:-1]])
    subdiagonal = jnp.where(degrees > order_value + 1.0, -factor / earlier_factor, 0.0)
    start_log = 0.5 * (
        lax.lgamma(order_value + 1.5) - lax.lgamma(jnp.float32(1.5)) - lax.lgamma(order_value + 1.0)
    ) - 0.5 * math.log(4.0 * math.pi)
    colatitude = (jnp.arange(lat_count, dtype=jnp.float32) + 0.5) * (math.pi / lat_count)
    cosine = jnp.cos(colatitude)[None, :]
    sines = jnp.sin(colatitude)
    block_len = 16
    block_count = degree_count // block_len
    grid_shape = (block_count, lat_count)

    def picked(values, step):
        return values.reshape(block_count, block_len)[:, step][:, None]

    def element(step):
        inside = picked(beyond, step)
        return (
            jnp.where(inside, 0.0, 1.0).astype(jnp.float32),
            jnp.where(inside, 1.0, 0.0).astype(jnp.float32),
            picked(subdiagonal, step),
            jnp.where(inside, picked(factor, step) * cosine, 1.0),
            jnp.zeros((block_count, 1), jnp.float32),
        )

    ones_grid = jnp.ones(grid_shape, jnp.float32)
    zeros_grid = jnp.zeros(grid_shape, jnp.float32)
    identity = (ones_grid, zeros_grid, zeros_grid, ones_grid, zeros_grid)
    totals = identity
    for step in range(block_len):
        totals = compose(totals, element(step))
    inclusive = lax.associative_scan(compose, totals, axis=0)
    carry = tuple(
        (
            jnp.concatenate([first[:1], later[:-1]], axis=0)
            for first, later in zip(identity, inclusive)
        )
    )
    lower_parts = []
    log_parts = []
    for step in range(block_len):
        carry = compose(carry, element(step))
        lower_parts.append(carry[3])
        log_parts.append(carry[4])
    lower_right = jnp.stack(lower_parts, axis=1).reshape(degree_count, lat_count)
    log_scale = jnp.stack(log_parts, axis=1).reshape(degree_count, lat_count)
    values = lower_right * jnp.exp(log_scale + start_log + order_value * jnp.log(sines)[None, :])
    functions = jnp.where((degrees >= order_value)[:, None], values, 0.0)
    weights = math.pi / lat_count * sines
    return (functions.astype(jnp.bfloat16), (functions * weights[None, :]).astype(jnp.bfloat16))


def halves(values):
    return jnp.split(values, 2, axis=1)


LAT_TILE = 16
SUB = 8


def kron_table(table, blocks):
    rows, points = table.shape
    height = rows // blocks
    index = jnp.arange(rows * SUB)
    source = index // (SUB * height) * height + index % height
    cycle = index // height % SUB
    point_of = jnp.arange(points * SUB)
    pick_row = (source[:, None] == jnp.arange(rows)[None, :]).astype(jnp.bfloat16)
    pick_point = (jnp.arange(points)[:, None] == point_of[None, :] // SUB).astype(jnp.bfloat16)
    wide = jnp.dot(table, pick_point, preferred_element_type=jnp.float32).astype(jnp.bfloat16)
    full = jnp.dot(pick_row, wide, preferred_element_type=jnp.float32)
    same = cycle[:, None] == point_of[None, :] % SUB
    return jnp.where(same, full, 0.0).astype(jnp.bfloat16)


def analyze_kernel(limit, factor, matrix_ref, grid_ref, out_ref):
    blocks, _, height, channels = out_ref.shape
    matrix = matrix_ref[...]
    values = grid_ref[...].astype(jnp.float32)
    for part in range(LAT_TILE // SUB):
        piece = values[:, part * SUB : (part + 1) * SUB]
        start = pl.program_id(0) * LAT_TILE + part * SUB
        cycle = start + lax.broadcasted_iota(jnp.int32, (1, SUB, 1), 1)
        piece = jnp.where(cycle < limit, piece, 0.0).reshape(-1, channels)
        product = jnp.dot(matrix, piece.astype(jnp.bfloat16), preferred_element_type=jnp.float32)
        product = (product * factor).reshape(blocks, SUB, height, channels).astype(jnp.bfloat16)
        out_ref[:, part * SUB : (part + 1) * SUB] = product


def synthesize_kernel(limit, factor, groups, matrix_ref, *refs):
    out_ref = refs[-1]
    points, _, channels = out_ref.shape
    matrix = matrix_ref[...]
    outs = []
    for part in range(LAT_TILE // SUB):
        here = slice(part * SUB, (part + 1) * SUB)
        start = pl.program_id(0) * LAT_TILE + part * SUB
        rows = []
        position = 0
        for size in groups:
            block = refs[position][:, here].astype(jnp.float32)
            for other in range(1, size):
                block = block + refs[position + other][:, here].astype(jnp.float32)
            position += size
            cycle = start + lax.broadcasted_iota(jnp.int32, (1, SUB, 1, 1), 1)
            rows.append(jnp.where(cycle < limit, block, 0.0).reshape(-1, channels))
        values = rows[0] if len(rows) == 1 else jnp.concatenate(rows, axis=0)
        product = jnp.dot(
            matrix, values.astype(jnp.bfloat16), preferred_element_type=jnp.float32
        )
        outs.append((product * factor).reshape(points, SUB, channels))
    out_ref[...] = jnp.concatenate(outs, axis=1).astype(jnp.bfloat16)


def grid_spec(points, channels):
    return pl.BlockSpec((points, LAT_TILE, channels), lambda step: (0, step, 0))


def piece_spec(blocks, height, channels):
    return pl.BlockSpec((blocks, LAT_TILE, height, channels), lambda step: (0, step, 0, 0))


def analyze_grid(table, grid, factor, blocks):
    points, lat_local, channels = grid.shape
    matrix = kron_table(table, blocks)
    height = table.shape[0] // blocks
    flops = 2 * matrix.size * channels * pl.cdiv(lat_local, SUB)
    return pl.pallas_call(
        lambda *refs: analyze_kernel(lat_local, factor, *refs),
        out_shape=jax.ShapeDtypeStruct((blocks, lat_local, height, channels), jnp.bfloat16),
        grid=(pl.cdiv(lat_local, LAT_TILE),),
        in_specs=[pl.BlockSpec(matrix.shape, lambda step: (0, 0)), grid_spec(points, channels)],
        out_specs=piece_spec(blocks, height, channels),
        compiler_params=pltpu.CompilerParams(vmem_limit_bytes=52 * 2**20),
        cost_estimate=pl.CostEstimate(
            flops=flops, bytes_accessed=2 * (grid.size + table.shape[0] * lat_local * channels), transcendentals=0
        ),
    )(matrix, grid)


def synthesize_grid(table, blocks, groups, factor):
    rows, points = table.shape
    pieces = [piece for group in groups for piece in group]
    _, lat_local, height, channels = pieces[0].shape
    matrix = kron_table(table, blocks).T
    flops = 2 * matrix.size * channels * pl.cdiv(lat_local, SUB)
    sizes = [len(group) for group in groups]
    return pl.pallas_call(
        lambda *refs: synthesize_kernel(lat_local, factor, sizes, *refs),
        out_shape=jax.ShapeDtypeStruct((points, lat_local, channels), jnp.bfloat16),
        grid=(pl.cdiv(lat_local, LAT_TILE),),
        in_specs=[pl.BlockSpec(matrix.shape, lambda step: (0, 0))]
        + [piece_spec(piece.shape[0], height, channels) for piece in pieces],
        out_specs=grid_spec(points, channels),
        compiler_params=pltpu.CompilerParams(vmem_limit_bytes=52 * 2**20),
        cost_estimate=pl.CostEstimate(
            flops=flops, bytes_accessed=2 * (points + rows) * lat_local * channels, transcendentals=0
        ),
    )(matrix, *pieces)


def pair_exchange(block, line, places):
    pairs = [(2 * z + y, 2 * z + 1 - y) for z in places for y in range(2)]
    return lax.ppermute(block, "lon", pairs)


def shift(block, places, step):
    pairs = [(2 * z + y, 2 * (z + step) + y) for z in places for y in range(2)]
    return lax.ppermute(block, "lon", pairs)


def line_gather(own, line):
    straight, crossed = {0: [own]}, {0: [pair_exchange(own, line, range(line))]}
    for offset in range(1, line):
        straight[offset], crossed[offset] = [], []
    upward, downward = own, own
    for step in range(1, line):
        upward = shift(upward, range(step - 1, line - 1), 1)
        downward = shift(downward, range(1, line - step + 1), -1)
        straight[line - step].append(upward)
        straight[step].append(downward)
        crossed[line - step].append(pair_exchange(upward, line, range(step, line)))
        crossed[step].append(pair_exchange(downward, line, range(0, line - step)))
    return [part[offset] for offset in range(line) for part in (straight, crossed)]


def per_device(field, cotangent, spectral_filter):
    lat_count = lax.axis_size("lat")
    lon_count = lax.axis_size("lon")
    lon_local, lat_local, channels = field.shape
    points = lon_local * lon_count
    latitudes = lat_local * lat_count
    wave_count = lat_count * lon_count
    degree_count = spectral_filter.shape[1]
    channel_share = channels // lon_count
    own_lon = lax.axis_index("lon")
    spacing = 2.0 * math.pi / points
    by_line = lon_count % 2 == 0 and lon_count <= 8
    line = lon_count // 2
    block_height = 2 * lat_count

    local_rows = lax.dynamic_slice_in_dim(
        fourier_table(wave_count, points), own_lon * lon_local, lon_local, 1
    )
    doubling = jnp.where(jnp.arange(2 * wave_count) // 2 == 0, 1.0, 2.0).astype(jnp.bfloat16)
    doubled_rows = local_rows * doubling[:, None]
    place, side = own_lon // 2, own_lon % 2

    def arranged(rows):
        targets = [
            2 * ((place + offset) % line) + (side + turn) % 2
            for offset in range(line)
            for turn in range(2)
        ]
        return jnp.concatenate(
            [
                lax.dynamic_slice_in_dim(rows, target * block_height, block_height, 0)
                for target in targets
            ]
        )

    filter_copies = jnp.broadcast_to(
        spectral_filter.reshape(1, -1, 128), (lon_count, spectral_filter.size // 128, 128)
    )
    filter_parts = lax.all_to_all(filter_copies, "lon", split_axis=0, concat_axis=0, tiled=True)
    weights = jnp.transpose(
        filter_parts.reshape(lon_count, 2, degree_count, channel_share), (1, 2, 0, 3)
    ).reshape(2, degree_count, channels)

    wave_order = own_lon * lat_count + lax.axis_index("lat")
    legendre, weighted = legendre_pair(wave_order, latitudes, degree_count)

    def longitude_sums(grid, rows, factor):
        partial = analyze_grid(rows, grid, factor, lon_count).reshape(-1, channels)
        return lax.psum_scatter(partial, "lon", scatter_dimension=0, tiled=True)

    def to_spectral(own):
        own = own.reshape(lat_local, lat_count, 2 * channels)
        own = jnp.transpose(own, (1, 0, 2))
        moved = lax.all_to_all(own, "lat", split_axis=0, concat_axis=0, tiled=True)
        return moved.reshape(latitudes, 2 * channels)

    def to_bands(spectra):
        bands = spectra.reshape(lat_count, lat_local, 2 * channels)
        moved = lax.all_to_all(bands, "lat", split_axis=0, concat_axis=0, tiled=True)
        return jnp.transpose(moved, (1, 0, 2)).reshape(lat_local, block_height, channels)

    def gathered(bands):
        rows = lax.all_gather(bands.reshape(-1, channels), "lon", axis=0, tiled=True)
        return [[rows.reshape(lon_count, lat_local, block_height, channels)]]

    field_sums = longitude_sums(field, local_rows, spacing)
    doubled_rows, weights = lax.optimization_barrier((doubled_rows, weights))
    weights = weights.astype(jnp.float32)
    cotangent_sums = longitude_sums(cotangent, doubled_rows, 1.0)

    analysis = jnp.dot(weighted, to_spectral(field_sums), preferred_element_type=jnp.float32)
    real, imaginary = halves(analysis)
    filtered = jnp.concatenate(
        [weights[0] * real - weights[1] * imaginary, weights[0] * imaginary + weights[1] * real],
        axis=1,
    ).astype(jnp.bfloat16)
    over_degrees = (((0,), (0,)), ((), ()))
    synthesis = lax.dot_general(
        legendre, filtered, over_degrees, preferred_element_type=jnp.float32
    ).astype(jnp.bfloat16)
    bands = to_bands(synthesis)
    if by_line:
        output_groups = line_gather(bands[None], line)
    else:
        output_groups = gathered(bands)
    cotangent_sums, output_groups = lax.optimization_barrier((cotangent_sums, output_groups))

    adjoint = jnp.dot(legendre, to_spectral(cotangent_sums), preferred_element_type=jnp.float32)
    adjoint_real, adjoint_imaginary = halves(adjoint)
    adjoint_filtered = jnp.concatenate(
        [
            weights[0] * adjoint_real + weights[1] * adjoint_imaginary,
            weights[0] * adjoint_imaginary - weights[1] * adjoint_real,
        ],
        axis=1,
    ).astype(jnp.bfloat16)
    adjoint_analysis = lax.dot_general(
        weighted, adjoint_filtered, over_degrees, preferred_element_type=jnp.float32
    ).astype(jnp.bfloat16)
    gradient_groups = gathered(to_bands(adjoint_analysis))

    output_rows = arranged(doubled_rows) if by_line else doubled_rows
    output = synthesize_grid(output_rows, lon_count, output_groups, 1.0)

    gradient_term = jnp.concatenate(
        [
            real * adjoint_real + imaginary * adjoint_imaginary,
            real * adjoint_imaginary - imaginary * adjoint_real,
        ],
        axis=1,
    )
    degree_share = degree_count // lat_count
    by_degree = gradient_term.reshape(lat_count, degree_share, 2 * channels)
    by_degree = lax.all_to_all(by_degree, "lat", split_axis=0, concat_axis=0, tiled=True).sum(0)
    by_channel = jnp.transpose(
        by_degree.reshape(degree_share, 2, lon_count, channel_share), (2, 1, 0, 3)
    ).reshape(lon_count, -1)
    by_channel = lax.all_to_all(by_channel, "lon", split_axis=0, concat_axis=0, tiled=True).sum(0)
    shares = lax.all_gather(by_channel, "lat", axis=0).reshape(
        lat_count, 2, degree_share, channel_share
    )
    grad_filter = jnp.transpose(shares, (1, 0, 2, 3)).reshape(2, degree_count, channel_share)
    grad_field = synthesize_grid(local_rows, lon_count, gradient_groups, spacing)
    return (output, grad_field, grad_filter)


def solution(mesh):
    in_specs = (P("lon", "lat", None), P("lon", "lat", None), P(None, None, "lon"))
    out_specs = (P("lon", "lat", None), P("lon", "lat", None), P(None, None, "lon"))
    return jax.shard_map(
        per_device, mesh=mesh, in_specs=in_specs, out_specs=out_specs, check_vma=False
    )
```
